32 devices in a mesh: parts: 2 (over y), db: 4 (over z), blk: 4 (over x, core).
Axes of the slice: x: 2, y: 2, z: 4, core: 2. Of those that a mesh axis runs over, the one named last changes fastest.
Arguments:
- queries: bfloat16 [8192, 768], P(('parts', 'db', 'blk')), parts along dimension 0, may hold values from -6 to 6
- projection: bfloat16 [768, 768], replicated, may hold values from -0.21875 to 0.21875
- vectors: bfloat16 [768, 32768], P(None, ('parts', 'db', 'blk')), parts along dimension 1, may hold values from -0.21875 to 0.21875
- bins: int32 [32768], P(('parts', 'db', 'blk')), parts along dimension 0, may hold values from 0 to 127, as said below
- routes: int32 [8192, 1], P(('parts', 'db', 'blk')), parts along dimension 0, may hold values from 0 to 3; in each aligned block of 256 rows (0 to 255, 256 to 511, ...) at most 128 rows name the same one
Outputs:
- best: float32 [8192, 128], P(('parts', 'db', 'blk')), parts along dimension 0
The draws below stay inside these ranges and needn't reach their ends.
There are 2 independent parts, one for each index of `parts`. The reference program is written for one: setup_inputs(seed, part) draws one part's arguments, and reference() takes and returns one part's arrays. A program takes and returns all parts, laid end to end along the dimension named above; an argument that names none is the same for every part. Nothing has to cross between parts.
Inputs may be any that keep to these rules, and one draw needn't show every extreme that they name: Within every aligned block of 1024 entries each of the 128 bins occurs exactly 1024 // 128 times. `routes`: within every aligned block of 256 rows no group is named by more than 128 rows; in every draw some block names some group exactly 128 times.
All inputs are finite; a program needn't handle non-finite values.
Results may differ from the reference program's by a relative error of at most 0.0014.
Values may be sent and summed in bfloat16 or wider, within the bound.
No kernel may reach another device: no remote copies, remote signals or barrier semaphores. Data moves between devices by JAX's collectives and lax.ppermute only.
A program may use at most 64 MiB of HBM per device.

```python
import math
import jax
import jax.numpy as jnp
import numpy as np
from jax import lax

D = 768
BINS = 128
REQ_DEV = 256
VEC_DEV = 1024
CAP = 128
REQUESTS = 4096
VECTORS = 16384
N_DB = 4
N_BLK = 4


def draw_bins(key, part):
    blocks_total = VECTORS // VEC_DEV
    block_keys = jax.random.split(jax.random.fold_in(key, 7), blocks_total)
    pattern = jnp.arange(VEC_DEV, dtype=jnp.int32) % BINS

    def shuffle_block(block_key):
        return jax.random.permutation(block_key, pattern)
    return jax.vmap(shuffle_block)(block_keys).reshape(-1)


def level_of(key, dims, shards, smallest, high):
    def one(dim, shards_of):
        steps = jax.random.uniform(jax.random.fold_in(jax.random.fold_in(key, 6), dim), (shards_of,), jnp.float32, smallest / len(shards), high / len(shards))
        return jnp.repeat(jnp.exp(steps), dims[dim] // shards_of).reshape((-1,) + (1,) * (len(dims) - dim - 1))

    level = one(*shards[0])
    for cut in shards[1:]:
        level = level * one(*cut)
    return level


def assign_block(stream_key, own, number, rows, count, top, limit, slope):
    order = jax.random.permutation(stream_key, count)
    packed, usual = portions_of(count, rows * top, limit, slope, True), portions_of(count, rows * top, limit, slope, False)
    places = jnp.arange(count)

    def named(sizes, offset_by):
        used = int((sizes > 0).sum())
        fixed = max(1, used // 4)
        shifted = fixed + (places - fixed + offset_by * (used - fixed)) % max(1, count - fixed)
        return jnp.zeros((count,), jnp.int32).at[order[jnp.where(places < fixed, places, shifted)]].set(jnp.asarray(sizes, jnp.int32))

    sizes = jnp.where(number % 4 == 0, named(packed, number // 4), named(usual, number - number // 4 - 1))
    mixed = jax.random.permutation(jax.random.fold_in(own, 3), count)
    source_of, receiver = mixed[0:count // 2 * 2:2], mixed[1:count // 2 * 2:2]
    margin = jnp.minimum(sizes[source_of] - 1, limit - sizes[receiver]) // 2
    margin = jnp.where((source_of == order[0]) | (receiver == order[0]) | (sizes[receiver] == 0), 0, jnp.maximum(margin, 0))
    shifted = jax.random.randint(jax.random.fold_in(own, 4), (count // 2,), 0, 1 << 20) % (margin + 1)
    sizes = sizes.at[source_of].add(-shifted).at[receiver].add(shifted)
    items = jnp.searchsorted(jnp.cumsum(sizes), jnp.arange(rows * top), side="right").astype(jnp.int32)
    table = items.reshape(top, rows).T
    table = table[jax.random.permutation(jax.random.fold_in(own, 1), rows)]
    offset_by = jax.random.randint(jax.random.fold_in(own, 2), (rows, 1), 0, top)
    return jnp.take_along_axis(table, (jnp.arange(top)[None, :] + offset_by) % top, axis=1)


def portions_of(count, total, bound, skew, full):
    portions = [(1 << 20) // math.isqrt(grade ** skew) + 1 for grade in range(1, count + 1)]
    largest = bound if full else min(bound, max(-(-total // count), total * portions[0] // sum(portions)))
    least = 1 if total - largest >= count - 1 else 0
    holding, rest = [largest] + [least] * (count - 1), total - largest - least * (count - 1)
    while rest > 0:
        movable = [i for i in range(1, count) if holding[i] < largest] or [i for i in range(1, count) if holding[i] < bound]
        mass, left = sum([portions[i] for i in movable]), rest
        for i in movable:
            addition = min(bound - holding[i], max(1, left * portions[i] // mass), rest)
            holding[i] = holding[i] + addition
            rest = rest - addition
    return np.array(holding)


def scatter_about(own_key, shape, scale, limit, shards=(), kind=jnp.bfloat16):
    drawn = scale * jax.random.normal(own_key, shape, jnp.float32)
    if shards:
        drawn = drawn * level_of(own_key, shape, shards, -0.22, 0.18)
    return jnp.clip(drawn, -limit, limit).astype(kind)


def setup_inputs(seed: int = 0, part: int = 0) -> dict:
    streams_of = jax.random.split(jax.random.key(seed), 6)
    part_keys = jax.random.split(jax.random.fold_in(streams_of[5], part), 6)
    queries = scatter_about(part_keys[0], (REQUESTS, D), 1.0, 6.0, ((0, 16),))
    projection = scatter_about(streams_of[1], (D, D), D ** -0.5, 0.21875)
    vectors = scatter_about(part_keys[2], (D, VECTORS), (D ** -0.5), 0.21875, ((1, 16),))
    bins = draw_bins(jax.random.fold_in(jax.random.fold_in(streams_of[5], part), 71), part)
    routes_keys = jax.random.split(jax.random.fold_in(part_keys[4], 1), REQUESTS // REQ_DEV)
    routes_turns = jax.random.permutation(jax.random.fold_in(part_keys[4], 3), REQUESTS // REQ_DEV)
    routes = jax.vmap(lambda own, number: assign_block(jax.random.fold_in(part_keys[4], 2), own, number, REQ_DEV, N_DB, 1, CAP, 2))(routes_keys, routes_turns).reshape((REQUESTS, 1))
    return {"queries": queries, "projection": projection, "vectors": vectors, "bins": bins, "routes": routes}


logit_scale = 10.0

def reference(queries, projection, vectors, bins, routes):
    devices_all = N_DB * N_BLK
    capacity = 2 * REQ_DEV // N_DB
    per_bin = VEC_DEV // BINS
    projected = jnp.dot(queries, projection, preferred_element_type=jnp.float32)
    normed = (projected * lax.rsqrt(lax.optimization_barrier(jnp.sum(projected * projected, axis=1, keepdims=True)) + 1e-06)).astype(jnp.bfloat16)
    target = routes[:, 0].reshape(devices_all, REQ_DEV)
    one_hot = (target[:, :, None] == jnp.arange(N_DB, dtype=jnp.int32)[None, None, :]).astype(jnp.int32)
    slot_index = lax.optimization_barrier(jnp.sum((jnp.cumsum(one_hot, axis=1) - one_hot) * one_hot, axis=2))
    requester = jnp.arange(devices_all, dtype=jnp.int32)[:, None]
    position = (target * (devices_all * capacity) + requester * capacity + slot_index).reshape(-1).astype(jnp.int32)
    dispatched = jnp.zeros((N_DB * devices_all * capacity, D), jnp.float32).at[position].set(normed.astype(jnp.float32))
    dispatched = dispatched.reshape(N_DB, devices_all * capacity, D)
    slab_all = vectors.reshape(D, devices_all, VEC_DEV)
    ordering = jnp.argsort(bins.reshape(devices_all, VEC_DEV), axis=1, stable=True).astype(jnp.int32)
    ordering = ordering.reshape(devices_all, BINS, per_bin).transpose(0, 2, 1).reshape(devices_all, VEC_DEV)
    sorted_all = jnp.take_along_axis(slab_all, ordering[None, :, :], axis=2)
    sorted_all = sorted_all.reshape(D, N_DB, N_BLK * VEC_DEV).transpose(1, 0, 2)

    def group_max(operands):
        query_rows, group_slab = operands
        scores = jnp.dot(query_rows, group_slab.astype(jnp.float32), preferred_element_type=jnp.float32)
        return logit_scale * lax.optimization_barrier(jnp.max(scores.reshape(query_rows.shape[0], N_BLK * per_bin, BINS), axis=1))
    maxima = lax.map(group_max, (dispatched, sorted_all))
    return maxima.reshape(-1, BINS)[position]
```

```python
import functools

import jax
import jax.numpy as jnp
from jax import lax
from jax.experimental import pallas as pl
from jax.experimental.pallas import tpu as pltpu
from jax.sharding import PartitionSpec as P

BINS = 128
logit_scale = 10.0
VMEM_LIMIT = 48 * 2**20


def params():
    return pltpu.CompilerParams(vmem_limit_bytes=VMEM_LIMIT)


def cost(flops, bytes_accessed):
    return pl.CostEstimate(flops=flops, bytes_accessed=bytes_accessed, transcendentals=0)


def ranks(member):
    count = member.shape[1]
    row = lax.broadcasted_iota(jnp.int32, (count, count), 0)
    column = lax.broadcasted_iota(jnp.int32, (count, count), 1)
    earlier = jnp.where(row < column, 1.0, 0.0).astype(jnp.bfloat16)
    seen = jnp.dot(member.astype(jnp.bfloat16), earlier, preferred_element_type=jnp.float32)
    return jnp.sum(seen * member, axis=0, keepdims=True).astype(jnp.int32)


def prepare_kernel(groups, capacity, me_ref, queries_ref, projection_ref, routes_ref, position_ref, *piece_refs):
    requests = queries_ref.shape[0]
    distance = jnp.bitwise_xor(routes_ref[...], me_ref[0, 0])
    classes = lax.broadcasted_iota(jnp.int32, (-(-groups // 8) * 8, requests), 0)
    member = jnp.where(classes == distance, 1.0, 0.0)
    position = distance * capacity + ranks(member)
    position_ref[...] = position
    projected = jnp.dot(queries_ref[...], projection_ref[...], preferred_element_type=jnp.float32)
    normed = (
        projected * lax.rsqrt(jnp.sum(projected * projected, axis=1, keepdims=True) + 1e-06)
    ).astype(jnp.bfloat16)
    slots = lax.broadcasted_iota(jnp.int32, (groups * capacity, requests), 0)
    chooser = jnp.where(slots == position, 1.0, 0.0).astype(jnp.bfloat16)
    outgoing = jnp.dot(chooser, normed, preferred_element_type=jnp.float32).astype(jnp.bfloat16)
    start = 0
    for ref in piece_refs:
        ref[...] = outgoing[start : start + ref.shape[0]]
        start += ref.shape[0]


def prepare(me, queries, projection, routes, groups, capacity, sizes):
    requests, width = queries.shape
    return pl.pallas_call(
        functools.partial(prepare_kernel, groups, capacity),
        out_shape=[jax.ShapeDtypeStruct((1, requests), jnp.int32)]
        + [jax.ShapeDtypeStruct((size, width), jnp.bfloat16) for size in sizes],
        in_specs=[pl.BlockSpec(memory_space=pltpu.SMEM)] + [pl.BlockSpec(memory_space=pltpu.VMEM)] * 3,
        compiler_params=params(),
        cost_estimate=cost(2 * requests * width * (width + groups * capacity), 3 * width * width),
        name="prepare",
    )(me.reshape(1, 1), queries, projection, routes.reshape(1, requests))


def sort_kernel(bins_ref, vectors_ref, sorted_ref):
    bins = bins_ref[...]
    width = bins.shape[1]
    classes = lax.broadcasted_iota(jnp.int32, (BINS, width), 0)
    member = jnp.where(classes == bins, 1.0, 0.0)
    position = ranks(member) * BINS + bins
    places = lax.broadcasted_iota(jnp.int32, (width, width), 0)
    chooser = jnp.where(places == position, 1.0, 0.0).astype(jnp.bfloat16)
    sorted_ref[...] = lax.dot_general(
        vectors_ref[...], chooser, (((1,), (1,)), ((), ())), preferred_element_type=jnp.float32
    ).astype(jnp.bfloat16)


def sort_slab(bins, vectors):
    depth, width = vectors.shape
    return pl.pallas_call(
        sort_kernel,
        out_shape=jax.ShapeDtypeStruct(vectors.shape, jnp.bfloat16),
        in_specs=[pl.BlockSpec(memory_space=pltpu.VMEM)] * 2,
        compiler_params=params(),
        cost_estimate=cost(2 * width * width * (depth + BINS), 4 * depth * width),
        name="sort_slab",
    )(bins.reshape(1, width), vectors)


def score_kernel(pieces, *refs):
    piece_refs, slab_refs, out_refs = refs[:pieces], refs[pieces:-pieces], refs[-pieces:]
    rows = jnp.concatenate([ref[...] for ref in piece_refs], axis=0)
    best = None
    step = 2 * BINS
    for slab_ref in slab_refs:
        for start in range(0, slab_ref.shape[1], step):
            scores = jnp.dot(rows, slab_ref[:, start : start + step], preferred_element_type=jnp.float32)
            for first in range(0, step, BINS):
                part = scores[:, first : first + BINS]
                best = part if best is None else jnp.maximum(best, part)
    start = 0
    for ref in out_refs:
        ref[...] = best[start : start + ref.shape[0]]
        start += ref.shape[0]


def score(pieces, slabs):
    rows = sum(piece.shape[0] for piece in pieces)
    columns = sum(slab.shape[1] for slab in slabs)
    width = slabs[0].shape[0]
    return pl.pallas_call(
        functools.partial(score_kernel, len(pieces)),
        out_shape=[jax.ShapeDtypeStruct((piece.shape[0], BINS), jnp.float32) for piece in pieces],
        in_specs=[pl.BlockSpec(memory_space=pltpu.VMEM)] * (len(pieces) + len(slabs)),
        compiler_params=params(),
        cost_estimate=cost(2 * rows * columns * width, 2 * width * (rows + columns)),
        name="score",
    )(*pieces, *slabs)


def select_kernel(position_ref, *refs):
    *answer_refs, out_ref = refs
    half = len(answer_refs) // 2
    answers = jnp.concatenate(
        [jnp.maximum(a[...], b[...]) for a, b in zip(answer_refs[:half], answer_refs[half:])], axis=0
    )
    high = answers.astype(jnp.bfloat16)
    rest = answers - high.astype(jnp.float32)
    middle = rest.astype(jnp.bfloat16)
    low = (rest - middle.astype(jnp.float32)).astype(jnp.bfloat16)
    parts = jnp.concatenate([high, middle, low], axis=1)
    position = position_ref[...]
    slots = lax.broadcasted_iota(jnp.int32, (answers.shape[0], position.shape[1]), 0)
    chooser = jnp.where(slots == position, 1.0, 0.0).astype(jnp.bfloat16)
    chosen = lax.dot_general(chooser, parts, (((0,), (0,)), ((), ())), preferred_element_type=jnp.float32)
    total = (chosen[:, :BINS] + chosen[:, BINS : 2 * BINS]) + chosen[:, 2 * BINS :]
    out_ref[...] = logit_scale * total


def select(position, first, second):
    requests = position.shape[1]
    slots = sum(a.shape[0] for a in first)
    return pl.pallas_call(
        select_kernel,
        out_shape=jax.ShapeDtypeStruct((requests, BINS), jnp.float32),
        in_specs=[pl.BlockSpec(memory_space=pltpu.VMEM)] * (1 + len(first) + len(second)),
        compiler_params=params(),
        cost_estimate=cost(6 * requests * slots * BINS, 8 * slots * BINS),
        name="select",
    )(position, *first, *second)


def device_paired(queries, projection, vectors, bins, routes):
    groups, slabs = lax.axis_size("db"), lax.axis_size("blk")
    requests = queries.shape[0]
    capacity = 2 * requests // groups
    me = lax.axis_index("db")

    def along_db(value, distance):
        return lax.ppermute(value, "db", [(i, i ^ distance) for i in range(groups)])

    def along_blk(value, distance):
        return lax.ppermute(value, "blk", [(i, i ^ distance) for i in range(slabs)])

    def along_both(value, distance, distance_blk):
        pairs = [
            (i * slabs + j, (i ^ distance) * slabs + (j ^ distance_blk))
            for i in range(groups)
            for j in range(slabs)
        ]
        return lax.ppermute(value, ("db", "blk"), pairs)

    position, *pieces = prepare(me, queries, projection, routes, groups, capacity, [capacity] * groups)
    order = [3, 1, 2]
    arrived = {0: pieces[0]}
    for distance in order:
        arrived[distance] = along_db(pieces[distance], distance)
    own_slab = sort_slab(bins, vectors)
    both_slabs = (own_slab, along_blk(own_slab, 1))
    first, second = {}, {}
    for distance in [0, 1, 3, 2]:
        partner = along_blk(arrived[distance], 2)
        here, there = score([arrived[distance], partner], both_slabs)
        if distance:
            first[distance] = along_db(here, distance)
            second[distance] = along_both(there, distance, 2)
        else:
            first[distance] = here
            second[distance] = along_blk(there, 2)
    ids = range(groups)
    return select(position, [first[k] for k in ids], [second[k] for k in ids])


def binned_max(query_rows, columns):
    scores = jnp.dot(query_rows, columns, preferred_element_type=jnp.float32)
    return jnp.max(scores.reshape(query_rows.shape[0], -1, BINS), axis=1)


def device_gathered(queries, projection, vectors, bins, routes):
    groups = lax.axis_size("db")
    requests = queries.shape[0]
    capacity = 2 * requests // groups
    slab_width = vectors.shape[1]
    per_bin = slab_width // BINS
    projected = jnp.dot(queries, projection, preferred_element_type=jnp.float32)
    normed = (
        projected * lax.rsqrt(jnp.sum(projected * projected, axis=1, keepdims=True) + 1e-06)
    ).astype(jnp.bfloat16)
    target = routes[:, 0]
    one_hot = (target[:, None] == jnp.arange(groups, dtype=jnp.int32)[None, :]).astype(jnp.int32)
    slot_index = jnp.sum((jnp.cumsum(one_hot, axis=0) - one_hot) * one_hot, axis=1)
    position = target * capacity + slot_index
    chooser = (jnp.arange(groups * capacity, dtype=jnp.int32)[:, None] == position[None, :]).astype(
        jnp.bfloat16
    )
    outgoing = jnp.dot(chooser, normed, preferred_element_type=jnp.float32).astype(jnp.bfloat16)
    arrived = lax.all_to_all(outgoing, "db", split_axis=0, concat_axis=0, tiled=True)
    ordering = jnp.argsort(bins, stable=True).reshape(BINS, per_bin).T.reshape(-1)
    sorted_slab = jnp.take(vectors, ordering, axis=1)
    maxima = binned_max(arrived, lax.all_gather(sorted_slab, "blk", axis=1, tiled=True))
    answers = lax.all_to_all(logit_scale * maxima, "db", split_axis=0, concat_axis=0, tiled=True)
    return jnp.take(answers, position, axis=0)


def solution(mesh):
    paired = mesh.shape["db"] == 4 and mesh.shape["blk"] == 4
    in_specs = (
        P(("parts", "db", "blk"), None),
        P(),
        P(None, ("parts", "db", "blk")),
        P(("parts", "db", "blk")),
        P(("parts", "db", "blk"), None),
    )
    out_specs = P(("parts", "db", "blk"), None)
    return jax.shard_map(
        device_paired if paired else device_gathered,
        mesh=mesh,
        in_specs=in_specs,
        out_specs=out_specs,
        check_vma=False,
    )
```

```python
import functools

import jax
import jax.numpy as jnp
from jax import lax
from jax.experimental import pallas as pl
from jax.experimental.pallas import tpu as pltpu
from jax.sharding import PartitionSpec as P

BINS = 128
logit_scale = 10.0
ORDER = (3, 1, 2)
PREP_LIMIT = 63 * 2**20
NO_COST = pl.CostEstimate(flops=0, bytes_accessed=0, transcendentals=0)
VMEM_LIMIT = 48 * 2**20


def params():
    return pltpu.CompilerParams(vmem_limit_bytes=VMEM_LIMIT)


def cost(flops, bytes_accessed):
    return pl.CostEstimate(flops=flops, bytes_accessed=bytes_accessed, transcendentals=0)


def ranks(member):
    count = member.shape[1]
    row = lax.broadcasted_iota(jnp.int32, (count, count), 0)
    column = lax.broadcasted_iota(jnp.int32, (count, count), 1)
    earlier = jnp.where(row < column, 1.0, 0.0).astype(jnp.bfloat16)
    seen = jnp.dot(member.astype(jnp.bfloat16), earlier, preferred_element_type=jnp.float32)
    return jnp.sum(seen * member, axis=0, keepdims=True).astype(jnp.int32)


def prepare_kernel(
    groups,
    capacity,
    sizes,
    queries_hbm,
    projection_hbm,
    routes_hbm,
    position_ref,
    *refs,
):
    piece_refs = refs[: len(sizes)]
    queries_ref, projection_ref, routes_ref, sems = refs[len(sizes) :]
    copies = [
        pltpu.make_async_copy(routes_hbm, routes_ref, sems.at[0]),
        pltpu.make_async_copy(projection_hbm, projection_ref, sems.at[1]),
        pltpu.make_async_copy(queries_hbm, queries_ref, sems.at[2]),
    ]
    for copy in copies:
        copy.start()
    requests = queries_ref.shape[0]
    me = lax.axis_index("db")
    copies[0].wait()
    distance = jnp.bitwise_xor(routes_ref[...], me)
    classes = lax.broadcasted_iota(jnp.int32, (-(-groups // 8) * 8, requests), 0)
    member = jnp.where(classes == distance, 1.0, 0.0)
    position = distance * capacity + ranks(member)
    position_ref[...] = position
    slots = lax.broadcasted_iota(jnp.int32, (groups * capacity, requests), 0)
    chooser = jnp.where(slots == position, 1.0, 0.0).astype(jnp.bfloat16)
    copies[1].wait()
    copies[2].wait()
    projected = jnp.dot(queries_ref[...], projection_ref[...], preferred_element_type=jnp.float32)
    normed = (
        projected * lax.rsqrt(jnp.sum(projected * projected, axis=1, keepdims=True) + 1e-06)
    ).astype(jnp.bfloat16)
    outgoing = jnp.dot(chooser, normed, preferred_element_type=jnp.float32).astype(jnp.bfloat16)
    start = 0
    for ref in piece_refs:
        ref[...] = outgoing[start : start + ref.shape[0]]
        start += ref.shape[0]


def prepare(queries, projection, routes, groups, capacity, sizes):
    requests, width = queries.shape
    return pl.pallas_call(
        functools.partial(prepare_kernel, groups, capacity, sizes),
        out_shape=[jax.ShapeDtypeStruct((1, requests), jnp.int32)]
        + [jax.ShapeDtypeStruct((size, width), jnp.bfloat16) for size in sizes],
        in_specs=[pl.BlockSpec(memory_space=pltpu.HBM)] * 3,
        scratch_shapes=[
            pltpu.VMEM(queries.shape, queries.dtype),
            pltpu.VMEM(projection.shape, projection.dtype),
            pltpu.VMEM((1, requests), jnp.int32),
            pltpu.SemaphoreType.DMA((3,)),
        ],
        compiler_params=pltpu.CompilerParams(vmem_limit_bytes=PREP_LIMIT),
        cost_estimate=cost(2 * requests * width * (width + groups * capacity), 3 * width * width),
        name="prepare",
    )(queries, projection, routes.reshape(1, requests))


def gate_kernel(value_ref, *refs):
    pass


def gate(value, *after):
    return pl.pallas_call(
        gate_kernel,
        out_shape=jax.ShapeDtypeStruct(value.shape, value.dtype),
        in_specs=[pl.BlockSpec(memory_space=pltpu.VMEM)] + [pl.BlockSpec(memory_space=pl.ANY)] * len(after),
        out_specs=pl.BlockSpec(memory_space=pltpu.VMEM),
        input_output_aliases={0: 0},
        compiler_params=params(),
        cost_estimate=NO_COST,
        name="gate",
    )(value, *after)


def sort_kernel(after_ref, *refs):
    slabs = len(refs) // 3
    row = lax.broadcasted_iota(jnp.int32, (BINS, BINS), 0)
    column = lax.broadcasted_iota(jnp.int32, (BINS, BINS), 1)
    earlier = jnp.where(row < column, 1.0, 0.0).astype(jnp.bfloat16)
    for bins_ref, slab_ref, sorted_ref in zip(refs[:slabs], refs[slabs : 2 * slabs], refs[2 * slabs :]):
        width = bins_ref.shape[1]
        places = lax.broadcasted_iota(jnp.int32, (width, BINS), 0)
        before = jnp.zeros((BINS, 1), jnp.float32)
        choosers = []
        for start in range(0, width, BINS):
            bins = bins_ref[:, start : start + BINS]
            member = jnp.where(row == bins, 1.0, 0.0)
            seen = before + jnp.dot(member.astype(jnp.bfloat16), earlier, preferred_element_type=jnp.float32)
            before += jnp.sum(member, axis=1, keepdims=True)
            rank = jnp.sum(seen * member, axis=0, keepdims=True).astype(jnp.int32)
            choosers.append(jnp.where(places == rank * BINS + bins, 1.0, 0.0).astype(jnp.bfloat16))
        sorted_ref[...] = lax.dot_general(
            slab_ref[...],
            jnp.concatenate(choosers, axis=1),
            (((1,), (1,)), ((), ())),
            preferred_element_type=jnp.float32,
        ).astype(jnp.bfloat16)


def sort_slabs(after, bins, slabs):
    depth, width = slabs[0].shape
    return pl.pallas_call(
        sort_kernel,
        out_shape=[jax.ShapeDtypeStruct(slab.shape, jnp.bfloat16) for slab in slabs],
        in_specs=[pl.BlockSpec(memory_space=pl.ANY)] + [pl.BlockSpec(memory_space=pltpu.VMEM)] * (2 * len(slabs)),
        compiler_params=params(),
        cost_estimate=NO_COST,
        name="sort_slabs",
    )(after, *[row.reshape(1, width) for row in bins], *slabs)


def score_kernel(afters, pieces, *refs):
    refs = refs[afters:]
    piece_refs, slab_refs, out_refs = refs[:pieces], refs[pieces:-pieces], refs[-pieces:]
    rows = jnp.concatenate([ref[...] for ref in piece_refs], axis=0)
    best = None
    step = 2 * BINS
    for slab_ref in slab_refs:
        for start in range(0, slab_ref.shape[1], step):
            scores = jnp.dot(rows, slab_ref[:, start : start + step], preferred_element_type=jnp.float32)
            for first in range(0, step, BINS):
                part = scores[:, first : first + BINS]
                best = part if best is None else jnp.maximum(best, part)
    start = 0
    for ref in out_refs:
        ref[...] = best[start : start + ref.shape[0]]
        start += ref.shape[0]


def score(after, pieces, slabs):
    rows = sum(piece.shape[0] for piece in pieces)
    columns = sum(slab.shape[1] for slab in slabs)
    width = slabs[0].shape[0]
    return pl.pallas_call(
        functools.partial(score_kernel, len(after), len(pieces)),
        out_shape=[jax.ShapeDtypeStruct((piece.shape[0], BINS), jnp.float32) for piece in pieces],
        in_specs=[pl.BlockSpec(memory_space=pl.ANY)] * len(after)
        + [pl.BlockSpec(memory_space=pltpu.VMEM)] * (len(pieces) + len(slabs)),
        compiler_params=params(),
        cost_estimate=cost(2 * rows * columns * width, 2 * width * (rows + columns)),
        name="score",
    )(*after, *pieces, *slabs)


def select_kernel(position_ref, *refs):
    *answer_refs, out_ref = refs
    half = len(answer_refs) // 2
    answers = jnp.concatenate(
        [jnp.maximum(a[...], b[...]) for a, b in zip(answer_refs[:half], answer_refs[half:])], axis=0
    )
    high = answers.astype(jnp.bfloat16)
    rest = answers - high.astype(jnp.float32)
    middle = rest.astype(jnp.bfloat16)
    low = (rest - middle.astype(jnp.float32)).astype(jnp.bfloat16)
    parts = jnp.concatenate([high, middle, low], axis=1)
    position = position_ref[...]
    slots = lax.broadcasted_iota(jnp.int32, (answers.shape[0], position.shape[1]), 0)
    chooser = jnp.where(slots == position, 1.0, 0.0).astype(jnp.bfloat16)
    chosen = lax.dot_general(chooser, parts, (((0,), (0,)), ((), ())), preferred_element_type=jnp.float32)
    total = (chosen[:, :BINS] + chosen[:, BINS : 2 * BINS]) + chosen[:, 2 * BINS :]
    out_ref[...] = logit_scale * total


def select(position, first, second):
    requests = position.shape[1]
    slots = sum(a.shape[0] for a in first)
    return pl.pallas_call(
        select_kernel,
        out_shape=jax.ShapeDtypeStruct((requests, BINS), jnp.float32),
        in_specs=[pl.BlockSpec(memory_space=pltpu.VMEM)] * (1 + len(first) + len(second)),
        compiler_params=params(),
        cost_estimate=cost(6 * requests * slots * BINS, 8 * slots * BINS),
        name="select",
    )(position, *first, *second)


def device_paired(queries, projection, vectors, bins, routes):
    groups, slabs = lax.axis_size("db"), lax.axis_size("blk")
    requests = queries.shape[0]
    capacity = 2 * requests // groups

    def along_db(value, distance):
        return lax.ppermute(value, "db", [(i, i ^ distance) for i in range(groups)])

    def along_blk(value, distance):
        return lax.ppermute(value, "blk", [(i, i ^ distance) for i in range(slabs)])

    def along_both(value, distance, distance_blk):
        pairs = [
            (i * slabs + j, (i ^ distance) * slabs + (j ^ distance_blk))
            for i in range(groups)
            for j in range(slabs)
        ]
        return lax.ppermute(value, ("db", "blk"), pairs)

    order = ORDER
    position, *pieces = prepare(queries, projection, routes, groups, capacity, [capacity] * groups)
    arrived, partner, results = {0: pieces[0]}, {}, {}
    for k in order:
        arrived[k] = along_db(pieces[k], k)
    partner[0] = along_blk(arrived[0], 2)
    slabs_here = sort_slabs(position, [bins, along_blk(bins, 1)], [vectors, along_blk(vectors, 1)])

    first, second = {}, {}

    def scores(k, *after):
        here, there = score(after, [arrived[k], partner[k]], slabs_here)
        results[k] = there
        first[k] = along_db(here, k) if k else here
        second[k] = along_both(there, k, 2) if k else along_blk(there, 2)

    a, b, c = order
    arrived[a] = gate(arrived[a], slabs_here[0])
    partner[a] = along_blk(arrived[a], 2)
    scores(0, arrived[a])
    arrived[b] = gate(arrived[b], second[0])
    partner[b] = along_blk(arrived[b], 2)
    partner[c] = along_blk(arrived[c], 2)
    scores(a, results[0])
    scores(b, results[a])
    scores(c, results[b], first[a])
    ids = range(groups)
    return select(position, [first[k] for k in ids], [second[k] for k in ids])


def binned_max(query_rows, columns):
    scores = jnp.dot(query_rows, columns, preferred_element_type=jnp.float32)
    return jnp.max(scores.reshape(query_rows.shape[0], -1, BINS), axis=1)


def device_gathered(queries, projection, vectors, bins, routes):
    groups = lax.axis_size("db")
    requests = queries.shape[0]
    capacity = 2 * requests // groups
    slab_width = vectors.shape[1]
    per_bin = slab_width // BINS
    projected = jnp.dot(queries, projection, preferred_element_type=jnp.float32)
    normed = (
        projected * lax.rsqrt(jnp.sum(projected * projected, axis=1, keepdims=True) + 1e-06)
    ).astype(jnp.bfloat16)
    target = routes[:, 0]
    one_hot = (target[:, None] == jnp.arange(groups, dtype=jnp.int32)[None, :]).astype(jnp.int32)
    slot_index = jnp.sum((jnp.cumsum(one_hot, axis=0) - one_hot) * one_hot, axis=1)
    position = target * capacity + slot_index
    chooser = (jnp.arange(groups * capacity, dtype=jnp.int32)[:, None] == position[None, :]).astype(
        jnp.bfloat16
    )
    outgoing = jnp.dot(chooser, normed, preferred_element_type=jnp.float32).astype(jnp.bfloat16)
    arrived = lax.all_to_all(outgoing, "db", split_axis=0, concat_axis=0, tiled=True)
    ordering = jnp.argsort(bins, stable=True).reshape(BINS, per_bin).T.reshape(-1)
    sorted_slab = jnp.take(vectors, ordering, axis=1)
    maxima = binned_max(arrived, lax.all_gather(sorted_slab, "blk", axis=1, tiled=True))
    answers = lax.all_to_all(logit_scale * maxima, "db", split_axis=0, concat_axis=0, tiled=True)
    return jnp.take(answers, position, axis=0)


def solution(mesh):
    paired = mesh.shape["db"] == 4 and mesh.shape["blk"] == 4
    in_specs = (
        P(("parts", "db", "blk"), None),
        P(),
        P(None, ("parts", "db", "blk")),
        P(("parts", "db", "blk")),
        P(("parts", "db", "blk"), None),
    )
    out_specs = P(("parts", "db", "blk"), None)
    return jax.shard_map(
        device_paired if paired else device_gathered,
        mesh=mesh,
        in_specs=in_specs,
        out_specs=out_specs,
        check_vma=False,
    )
```

```python
import functools

import jax
import jax.numpy as jnp
from jax import lax
from jax.experimental import pallas as pl
from jax.experimental.pallas import tpu as pltpu
from jax.sharding import PartitionSpec as P

BINS = 128
logit_scale = 10.0
MIB = 2**20


def params(limit=48):
    return pltpu.CompilerParams(vmem_limit_bytes=limit * MIB)


def us(time):
    return pl.CostEstimate(flops=int(time * 10**9), bytes_accessed=0, transcendentals=0)


def ranks(member):
    count = member.shape[1]
    row = lax.broadcasted_iota(jnp.int32, (count, count), 0)
    column = lax.broadcasted_iota(jnp.int32, (count, count), 1)
    earlier = jnp.where(row < column, 1.0, 0.0).astype(jnp.bfloat16)
    seen = jnp.dot(member.astype(jnp.bfloat16), earlier, preferred_element_type=jnp.float32)
    return jnp.sum(seen * member, axis=0, keepdims=True).astype(jnp.int32)


def sorted_columns(bins_row, slab):
    row = lax.broadcasted_iota(jnp.int32, (BINS, BINS), 0)
    column = lax.broadcasted_iota(jnp.int32, (BINS, BINS), 1)
    earlier = jnp.where(row < column, 1.0, 0.0).astype(jnp.bfloat16)
    width = bins_row.shape[1]
    places = lax.broadcasted_iota(jnp.int32, (width, BINS), 0)
    before = jnp.zeros((BINS, 1), jnp.float32)
    choosers = []
    for start in range(0, width, BINS):
        bins = bins_row[:, start : start + BINS]
        member = jnp.where(row == bins, 1.0, 0.0)
        seen = before + jnp.dot(member.astype(jnp.bfloat16), earlier, preferred_element_type=jnp.float32)
        before += jnp.sum(member, axis=1, keepdims=True)
        rank = jnp.sum(seen * member, axis=0, keepdims=True).astype(jnp.int32)
        choosers.append(jnp.where(places == rank * BINS + bins, 1.0, 0.0).astype(jnp.bfloat16))
    return lax.dot_general(
        slab, jnp.concatenate(choosers, axis=1), (((1,), (1,)), ((), ())), preferred_element_type=jnp.float32
    ).astype(jnp.bfloat16)


def projected_rows(queries, projection):
    projected = jnp.dot(queries, projection, preferred_element_type=jnp.float32)
    scale = lax.rsqrt(jnp.sum(projected * projected, axis=1, keepdims=True) + 1e-06)
    return (projected * scale).astype(jnp.bfloat16)


def prepare_kernel(groups, capacity, routes_hbm, queries_hbm, position_ref, *refs):
    piece_refs, (routes_ref, queries_ref, sems) = refs[:groups], refs[groups:]
    copies = [
        pltpu.make_async_copy(routes_hbm, routes_ref, sems.at[0]),
        pltpu.make_async_copy(queries_hbm, queries_ref, sems.at[1]),
    ]
    for copy in copies:
        copy.start()
    requests = queries_ref.shape[0]
    copies[0].wait()
    distance = jnp.bitwise_xor(routes_ref[...], lax.axis_index("db"))
    classes = lax.broadcasted_iota(jnp.int32, (-(-groups // 8) * 8, requests), 0)
    member = jnp.where(classes == distance, 1.0, 0.0)
    position = distance * capacity + ranks(member)
    position_ref[...] = position
    slots = lax.broadcasted_iota(jnp.int32, (groups * capacity, requests), 0)
    chooser = jnp.where(slots == position, 1.0, 0.0).astype(jnp.bfloat16)
    copies[1].wait()
    outgoing = jnp.dot(chooser, queries_ref[...], preferred_element_type=jnp.float32).astype(jnp.bfloat16)
    for i, ref in enumerate(piece_refs):
        ref[...] = outgoing[i * capacity : (i + 1) * capacity]


def prepare(queries, routes, groups, capacity):
    requests, width = queries.shape
    ins = [routes.reshape(1, requests), queries]
    return pl.pallas_call(
        functools.partial(prepare_kernel, groups, capacity),
        out_shape=[jax.ShapeDtypeStruct((1, requests), jnp.int32)]
        + [jax.ShapeDtypeStruct((capacity, width), jnp.bfloat16)] * groups,
        in_specs=[pl.BlockSpec(memory_space=pltpu.HBM)] * len(ins),
        scratch_shapes=[pltpu.VMEM(x.shape, x.dtype) for x in ins] + [pltpu.SemaphoreType.DMA((len(ins),))],
        compiler_params=params(63),
        cost_estimate=us(0),
        name="prepare",
    )(*ins)


def project_kernel(piece_ref, projection_ref, *refs):
    refs[-1][...] = projected_rows(piece_ref[...], projection_ref[...])


def project(piece, projection, *after):
    return pl.pallas_call(
        project_kernel,
        out_shape=jax.ShapeDtypeStruct(piece.shape, jnp.bfloat16),
        in_specs=[pl.BlockSpec(memory_space=pltpu.VMEM)] * 2 + [pl.BlockSpec(memory_space=pl.ANY)] * len(after),
        compiler_params=params(),
        cost_estimate=us(0),
        name="project",
    )(piece, projection, *after)


def sort_kernel(slabs, after_ref, *refs):
    for bins_ref, slab_ref, sorted_ref in zip(refs[:slabs], refs[slabs : 2 * slabs], refs[2 * slabs :]):
        sorted_ref[...] = sorted_columns(bins_ref[...], slab_ref[...])


def sort_slabs(after, bins, slabs):
    width = slabs[0].shape[1]
    return pl.pallas_call(
        functools.partial(sort_kernel, len(slabs)),
        out_shape=[jax.ShapeDtypeStruct(slab.shape, jnp.bfloat16) for slab in slabs],
        in_specs=[pl.BlockSpec(memory_space=pl.ANY)] + [pl.BlockSpec(memory_space=pltpu.VMEM)] * (2 * len(slabs)),
        compiler_params=params(),
        cost_estimate=us(0),
        name="sort_slabs",
    )(after, *[row.reshape(1, width) for row in bins], *slabs)


def score_kernel(afters, pieces, outs, *refs):
    refs = refs[afters:]
    piece_refs, slab_refs, out_refs = refs[:pieces], refs[pieces:-outs], refs[-outs:]
    rows = jnp.concatenate([ref[...] for ref in piece_refs], axis=0)
    best = None
    step = 2 * BINS
    for slab_ref in slab_refs:
        for start in range(0, slab_ref.shape[1], step):
            scores = jnp.dot(rows, slab_ref[:, start : start + step], preferred_element_type=jnp.float32)
            for first in range(0, step, BINS):
                part = scores[:, first : first + BINS]
                best = part if best is None else jnp.maximum(best, part)
    start = 0
    for ref in out_refs:
        ref[...] = best[start : start + ref.shape[0]]
        start += ref.shape[0]


def score(after, pieces, slabs, sizes):
    rows = sum(sizes)
    return pl.pallas_call(
        functools.partial(score_kernel, len(after), len(pieces), len(sizes)),
        out_shape=[jax.ShapeDtypeStruct((size, BINS), jnp.float32) for size in sizes],
        in_specs=[pl.BlockSpec(memory_space=pl.ANY)] * len(after)
        + [pl.BlockSpec(memory_space=pltpu.VMEM)] * (len(pieces) + len(slabs)),
        compiler_params=params(),
        cost_estimate=us(rows / 256),
        name="score",
    )(*after, *pieces, *slabs)


def select_kernel(pieces, position_ref, *refs):
    out_ref = refs[-1]
    answers = [jnp.maximum(a[...], b[...]) for a, b in zip(refs[:pieces], refs[pieces : 2 * pieces])]
    answers = jnp.concatenate(answers, axis=0)
    high = answers.astype(jnp.bfloat16)
    rest = answers - high.astype(jnp.float32)
    middle = rest.astype(jnp.bfloat16)
    low = (rest - middle.astype(jnp.float32)).astype(jnp.bfloat16)
    parts = jnp.concatenate([high, middle, low], axis=1)
    position = position_ref[...]
    slots = lax.broadcasted_iota(jnp.int32, (answers.shape[0], position.shape[1]), 0)
    chooser = jnp.where(slots == position, 1.0, 0.0).astype(jnp.bfloat16)
    chosen = lax.dot_general(chooser, parts, (((0,), (0,)), ((), ())), preferred_element_type=jnp.float32)
    out_ref[...] = logit_scale * ((chosen[:, :BINS] + chosen[:, BINS : 2 * BINS]) + chosen[:, 2 * BINS :])


def select(position, first, second):
    return pl.pallas_call(
        functools.partial(select_kernel, len(first)),
        out_shape=jax.ShapeDtypeStruct((position.shape[1], BINS), jnp.float32),
        in_specs=[pl.BlockSpec(memory_space=pltpu.VMEM)] * (1 + 2 * len(first)),
        compiler_params=params(),
        cost_estimate=us(0),
        name="select",
    )(position, *first, *second)


def device_paired(queries, projection, vectors, bins, routes):
    groups, slabs = lax.axis_size("db"), lax.axis_size("blk")
    requests = queries.shape[0]
    capacity = 2 * requests // groups

    def along_db(value, distance):
        return lax.ppermute(value, "db", [(i, i ^ distance) for i in range(groups)])

    def along_blk(value, distance):
        return lax.ppermute(value, "blk", [(i, i ^ distance) for i in range(slabs)])

    def along_both(value, distance, distance_blk):
        pairs = [
            (i * slabs + j, (i ^ distance) * slabs + (j ^ distance_blk))
            for i in range(groups)
            for j in range(slabs)
        ]
        return lax.ppermute(value, ("db", "blk"), pairs)

    position, *pieces = prepare(queries, routes, groups, capacity)
    arrived = {k: along_db(pieces[k], k) for k in (3, 1, 2)}
    slabs_here = sort_slabs(position, [bins, along_blk(bins, 1)], [vectors, along_blk(vectors, 1)])
    here = {0: project(pieces[0], projection)}
    for k in (3, 1, 2):
        here[k] = project(arrived[k], projection, slabs_here[0])
    partner = {k: along_blk(here[k], 2) for k in (0, 3, 1, 2)}
    first, second = {}, {}

    def scores(wave, *after):
        found = score(after, [here[k] for k in wave] + [partner[k] for k in wave], slabs_here, [capacity] * 2 * len(wave))
        for k, mine, theirs in zip(wave, found[: len(wave)], found[len(wave) :]):
            first[k] = along_db(mine, k) if k else mine
            second[k] = along_both(theirs, k, 2) if k else along_blk(theirs, 2)
        return found[-1]

    done = scores([3, 0])
    done = scores([1], done)
    scores([2], done, first[3], second[3], second[0])
    ids = range(groups)
    return select(position, [first[k] for k in ids], [second[k] for k in ids])


def binned_max(query_rows, columns):
    scores = jnp.dot(query_rows, columns, preferred_element_type=jnp.float32)
    return jnp.max(scores.reshape(query_rows.shape[0], -1, BINS), axis=1)


def device_gathered(queries, projection, vectors, bins, routes):
    groups = lax.axis_size("db")
    requests = queries.shape[0]
    capacity = 2 * requests // groups
    slab_width = vectors.shape[1]
    per_bin = slab_width // BINS
    projected = jnp.dot(queries, projection, preferred_element_type=jnp.float32)
    normed = (
        projected * lax.rsqrt(jnp.sum(projected * projected, axis=1, keepdims=True) + 1e-06)
    ).astype(jnp.bfloat16)
    target = routes[:, 0]
    one_hot = (target[:, None] == jnp.arange(groups, dtype=jnp.int32)[None, :]).astype(jnp.int32)
    slot_index = jnp.sum((jnp.cumsum(one_hot, axis=0) - one_hot) * one_hot, axis=1)
    position = target * capacity + slot_index
    chooser = (jnp.arange(groups * capacity, dtype=jnp.int32)[:, None] == position[None, :]).astype(
        jnp.bfloat16
    )
    outgoing = jnp.dot(chooser, normed, preferred_element_type=jnp.float32).astype(jnp.bfloat16)
    arrived = lax.all_to_all(outgoing, "db", split_axis=0, concat_axis=0, tiled=True)
    ordering = jnp.argsort(bins, stable=True).reshape(BINS, per_bin).T.reshape(-1)
    sorted_slab = jnp.take(vectors, ordering, axis=1)
    maxima = binned_max(arrived, lax.all_gather(sorted_slab, "blk", axis=1, tiled=True))
    answers = lax.all_to_all(logit_scale * maxima, "db", split_axis=0, concat_axis=0, tiled=True)
    return jnp.take(answers, position, axis=0)


def solution(mesh):
    paired = mesh.shape["db"] == 4 and mesh.shape["blk"] == 4
    in_specs = (
        P(("parts", "db", "blk"), None),
        P(),
        P(None, ("parts", "db", "blk")),
        P(("parts", "db", "blk")),
        P(("parts", "db", "blk"), None),
    )
    out_specs = P(("parts", "db", "blk"), None)
    return jax.shard_map(
        device_paired if paired else device_gathered,
        mesh=mesh,
        in_specs=in_specs,
        out_specs=out_specs,
        check_vma=False,
    )
```

```python
import functools

import jax
import jax.numpy as jnp
from jax import lax
from jax.experimental import pallas as pl
from jax.experimental.pallas import tpu as pltpu
from jax.sharding import PartitionSpec as P

BINS = 128
logit_scale = 10.0
MIB = 2**20


def params(limit=48):
    return pltpu.CompilerParams(vmem_limit_bytes=limit * MIB)


def us(time):
    return pl.CostEstimate(flops=int(time * 10**9), bytes_accessed=0, transcendentals=0)


def ranks(member):
    count = member.shape[1]
    row = lax.broadcasted_iota(jnp.int32, (count, count), 0)
    column = lax.broadcasted_iota(jnp.int32, (count, count), 1)
    earlier = jnp.where(row < column, 1.0, 0.0).astype(jnp.bfloat16)
    seen = jnp.dot(member.astype(jnp.bfloat16), earlier, preferred_element_type=jnp.float32)
    return jnp.sum(seen * member, axis=0, keepdims=True).astype(jnp.int32)


def sorted_columns(bins_row, slab):
    row = lax.broadcasted_iota(jnp.int32, (BINS, BINS), 0)
    column = lax.broadcasted_iota(jnp.int32, (BINS, BINS), 1)
    earlier = jnp.where(row < column, 1.0, 0.0).astype(jnp.bfloat16)
    width = bins_row.shape[1]
    places = lax.broadcasted_iota(jnp.int32, (width, BINS), 0)
    before = jnp.zeros((BINS, 1), jnp.float32)
    choosers = []
    for start in range(0, width, BINS):
        bins = bins_row[:, start : start + BINS]
        member = jnp.where(row == bins, 1.0, 0.0)
        seen = before + jnp.dot(member.astype(jnp.bfloat16), earlier, preferred_element_type=jnp.float32)
        before += jnp.sum(member, axis=1, keepdims=True)
        rank = jnp.sum(seen * member, axis=0, keepdims=True).astype(jnp.int32)
        choosers.append(jnp.where(places == rank * BINS + bins, 1.0, 0.0).astype(jnp.bfloat16))
    return lax.dot_general(
        slab, jnp.concatenate(choosers, axis=1), (((1,), (1,)), ((), ())), preferred_element_type=jnp.float32
    ).astype(jnp.bfloat16)


def projected_rows(queries, projection):
    projected = jnp.dot(queries, projection, preferred_element_type=jnp.float32)
    scale = lax.rsqrt(jnp.sum(projected * projected, axis=1, keepdims=True) + 1e-06)
    return (projected * scale).astype(jnp.bfloat16)


def prepare_kernel(groups, capacity, routes_hbm, queries_hbm, position_ref, *refs):
    piece_refs, (routes_ref, queries_ref, sems) = refs[:groups], refs[groups:]
    copies = [
        pltpu.make_async_copy(routes_hbm, routes_ref, sems.at[0]),
        pltpu.make_async_copy(queries_hbm, queries_ref, sems.at[1]),
    ]
    for copy in copies:
        copy.start()
    requests = queries_ref.shape[0]
    copies[0].wait()
    distance = jnp.bitwise_xor(routes_ref[...], lax.axis_index("db"))
    classes = lax.broadcasted_iota(jnp.int32, (-(-groups // 8) * 8, requests), 0)
    member = jnp.where(classes == distance, 1.0, 0.0)
    position = distance * capacity + ranks(member)
    position_ref[...] = position
    slots = lax.broadcasted_iota(jnp.int32, (groups * capacity, requests), 0)
    chooser = jnp.where(slots == position, 1.0, 0.0).astype(jnp.bfloat16)
    copies[1].wait()
    outgoing = jnp.dot(chooser, queries_ref[...], preferred_element_type=jnp.float32).astype(jnp.bfloat16)
    for i, ref in enumerate(piece_refs):
        ref[...] = outgoing[i * capacity : (i + 1) * capacity]


def prepare(queries, routes, groups, capacity):
    requests, width = queries.shape
    ins = [routes.reshape(1, requests), queries]
    return pl.pallas_call(
        functools.partial(prepare_kernel, groups, capacity),
        out_shape=[jax.ShapeDtypeStruct((1, requests), jnp.int32)]
        + [jax.ShapeDtypeStruct((capacity, width), jnp.bfloat16)] * groups,
        in_specs=[pl.BlockSpec(memory_space=pltpu.HBM)] * len(ins),
        scratch_shapes=[pltpu.VMEM(x.shape, x.dtype) for x in ins] + [pltpu.SemaphoreType.DMA((len(ins),))],
        compiler_params=params(63),
        cost_estimate=us(0),
        name="prepare",
    )(*ins)


def project_kernel(piece_ref, projection_ref, *refs):
    refs[-1][...] = projected_rows(piece_ref[...], projection_ref[...])


def project(piece, projection, *after):
    return pl.pallas_call(
        project_kernel,
        out_shape=jax.ShapeDtypeStruct(piece.shape, jnp.bfloat16),
        in_specs=[pl.BlockSpec(memory_space=pltpu.VMEM)] * 2 + [pl.BlockSpec(memory_space=pl.ANY)] * len(after),
        compiler_params=params(),
        cost_estimate=us(0),
        name="project",
    )(piece, projection, *after)


def sort_kernel(after_ref, bins_ref, slab_ref, other_bins_ref, other_hbm, sorted_ref, other_sorted_ref, other_ref, sem):
    copy = pltpu.make_async_copy(other_hbm, other_ref, sem)
    copy.start()
    sorted_ref[...] = sorted_columns(bins_ref[...], slab_ref[...])
    copy.wait()
    other_sorted_ref[...] = sorted_columns(other_bins_ref[...], other_ref[...])


def sort_slabs(after, bins, slab, other_bins, other_slab):
    width = slab.shape[1]
    vmem, hbm = pl.BlockSpec(memory_space=pltpu.VMEM), pl.BlockSpec(memory_space=pltpu.HBM)
    return pl.pallas_call(
        sort_kernel,
        out_shape=[jax.ShapeDtypeStruct(slab.shape, jnp.bfloat16)] * 2,
        in_specs=[pl.BlockSpec(memory_space=pl.ANY), vmem, vmem, vmem, hbm],
        scratch_shapes=[pltpu.VMEM(slab.shape, slab.dtype), pltpu.SemaphoreType.DMA],
        compiler_params=params(),
        cost_estimate=us(0),
        name="sort_slabs",
    )(after, bins.reshape(1, width), slab, other_bins.reshape(1, width), other_slab)


def score_kernel(afters, pieces, *refs):
    refs = refs[afters:]
    piece_refs, slab_refs, out_refs = refs[:pieces], refs[pieces : pieces + 2], refs[pieces + 2 :]
    rows = jnp.concatenate([ref[...] for ref in piece_refs], axis=0)
    best = None
    step = 2 * BINS
    for slab_ref in slab_refs:
        for start in range(0, slab_ref.shape[1], step):
            scores = jnp.dot(rows, slab_ref[:, start : start + step], preferred_element_type=jnp.float32)
            for first in range(0, step, BINS):
                part = scores[:, first : first + BINS]
                best = part if best is None else jnp.maximum(best, part)
    count = best.shape[0] // len(out_refs)
    for i, ref in enumerate(out_refs):
        ref[...] = best[i * count : (i + 1) * count]


def score(after, pieces, slabs):
    return pl.pallas_call(
        functools.partial(score_kernel, len(after), len(pieces)),
        out_shape=[jax.ShapeDtypeStruct((piece.shape[0], BINS), jnp.float32) for piece in pieces],
        in_specs=[pl.BlockSpec(memory_space=pl.ANY)] * len(after)
        + [pl.BlockSpec(memory_space=pltpu.VMEM)] * (len(pieces) + len(slabs)),
        compiler_params=params(),
        cost_estimate=us(0),
        name="score",
    )(*after, *pieces, *slabs)


def select_kernel(distances, position_ref, *refs):
    pieces = len(distances)
    first_refs, second_refs, others, out_ref = refs[:pieces], refs[pieces : 2 * pieces], refs[2 * pieces : -1], refs[-1]
    position = position_ref[...]
    parts, choosers = [], []
    for k, first_ref, second_ref in zip(distances, first_refs, second_refs):
        values = jnp.maximum(first_ref[...], second_ref[...])
        high = values.astype(jnp.bfloat16)
        rest = values - high.astype(jnp.float32)
        middle = rest.astype(jnp.bfloat16)
        low = (rest - middle.astype(jnp.float32)).astype(jnp.bfloat16)
        parts.append(jnp.concatenate([high, middle, low], axis=1))
        slots = lax.broadcasted_iota(jnp.int32, (values.shape[0], position.shape[1]), 0)
        choosers.append(jnp.where(slots + k * values.shape[0] == position, 1.0, 0.0).astype(jnp.bfloat16))
    chosen = lax.dot_general(
        jnp.concatenate(choosers, axis=0),
        jnp.concatenate(parts, axis=0),
        (((0,), (0,)), ((), ())),
        preferred_element_type=jnp.float32,
    )
    total = logit_scale * ((chosen[:, :BINS] + chosen[:, BINS : 2 * BINS]) + chosen[:, 2 * BINS :])
    for ref in others:
        total += ref[...]
    out_ref[...] = total


def select(position, distances, answers, others, time):
    flat = [answers[k][i] for i in (0, 1) for k in distances] + others
    return pl.pallas_call(
        functools.partial(select_kernel, distances),
        out_shape=jax.ShapeDtypeStruct((position.shape[1], BINS), jnp.float32),
        in_specs=[pl.BlockSpec(memory_space=pltpu.VMEM)] * (1 + len(flat)),
        compiler_params=params(),
        cost_estimate=us(time),
        name="select",
    )(position, *flat)


def device_paired(queries, projection, vectors, bins, routes):
    groups, slabs = lax.axis_size("db"), lax.axis_size("blk")
    requests = queries.shape[0]
    capacity = 2 * requests // groups

    def along_db(value, distance):
        return lax.ppermute(value, "db", [(i, i ^ distance) for i in range(groups)])

    def along_blk(value, distance):
        return lax.ppermute(value, "blk", [(i, i ^ distance) for i in range(slabs)])

    def along_both(value, distance, distance_blk):
        pairs = [
            (i * slabs + j, (i ^ distance) * slabs + (j ^ distance_blk))
            for i in range(groups)
            for j in range(slabs)
        ]
        return lax.ppermute(value, ("db", "blk"), pairs)

    position, *pieces = prepare(queries, routes, groups, capacity)
    other_slab, other_bins = along_blk(vectors, 1), along_blk(bins, 1)
    slabs_here = sort_slabs(position, bins, vectors, other_bins, other_slab)
    arrived = {k: along_db(pieces[k], k) for k in (3, 1, 2)}
    here, partner = {}, {}
    for k, piece, after in (
        (0, pieces[0], [other_bins]),
        (1, arrived[1], []),
        (3, arrived[3], []),
        (2, arrived[2], [slabs_here[0]]),
    ):
        here[k] = project(piece, projection, *after)
        partner[k] = along_blk(here[k], 2)
    answers, after = {}, []
    for wave in ((3, 0), (1,), (2,)):
        found = score(after, [here[k] for k in wave] + [partner[k] for k in wave], slabs_here)
        for k, mine, theirs in zip(wave, found[: len(wave)], found[len(wave) :]):
            answers[k] = (along_db(mine, k), along_both(theirs, k, 2)) if k else (mine, along_blk(theirs, 2))
        after = found[-1:]
    some = select(position, (3,), answers, [], 3)
    return select(position, (0, 1, 2), answers, [some], 0)


def binned_max(query_rows, columns):
    scores = jnp.dot(query_rows, columns, preferred_element_type=jnp.float32)
    return jnp.max(scores.reshape(query_rows.shape[0], -1, BINS), axis=1)


def device_gathered(queries, projection, vectors, bins, routes):
    groups = lax.axis_size("db")
    requests = queries.shape[0]
    capacity = 2 * requests // groups
    slab_width = vectors.shape[1]
    per_bin = slab_width // BINS
    projected = jnp.dot(queries, projection, preferred_element_type=jnp.float32)
    normed = (
        projected * lax.rsqrt(jnp.sum(projected * projected, axis=1, keepdims=True) + 1e-06)
    ).astype(jnp.bfloat16)
    target = routes[:, 0]
    one_hot = (target[:, None] == jnp.arange(groups, dtype=jnp.int32)[None, :]).astype(jnp.int32)
    slot_index = jnp.sum((jnp.cumsum(one_hot, axis=0) - one_hot) * one_hot, axis=1)
    position = target * capacity + slot_index
    chooser = (jnp.arange(groups * capacity, dtype=jnp.int32)[:, None] == position[None, :]).astype(
        jnp.bfloat16
    )
    outgoing = jnp.dot(chooser, normed, preferred_element_type=jnp.float32).astype(jnp.bfloat16)
    arrived = lax.all_to_all(outgoing, "db", split_axis=0, concat_axis=0, tiled=True)
    ordering = jnp.argsort(bins, stable=True).reshape(BINS, per_bin).T.reshape(-1)
    sorted_slab = jnp.take(vectors, ordering, axis=1)
    maxima = binned_max(arrived, lax.all_gather(sorted_slab, "blk", axis=1, tiled=True))
    answers = lax.all_to_all(logit_scale * maxima, "db", split_axis=0, concat_axis=0, tiled=True)
    return jnp.take(answers, position, axis=0)


def solution(mesh):
    paired = mesh.shape["db"] == 4 and mesh.shape["blk"] == 4
    in_specs = (
        P(("parts", "db", "blk"), None),
        P(),
        P(None, ("parts", "db", "blk")),
        P(("parts", "db", "blk")),
        P(("parts", "db", "blk"), None),
    )
    out_specs = P(("parts", "db", "blk"), None)
    return jax.shard_map(
        device_paired if paired else device_gathered,
        mesh=mesh,
        in_specs=in_specs,
        out_specs=out_specs,
        check_vma=False,
    )
```

```python
import functools

import jax
import jax.numpy as jnp
from jax import lax
from jax.experimental import pallas as pl
from jax.experimental.pallas import tpu as pltpu
from jax.sharding import PartitionSpec as P

BINS = 128
logit_scale = 10.0
MIB = 2**20


def params(limit=48):
    return pltpu.CompilerParams(vmem_limit_bytes=limit * MIB)


def us(time):
    return pl.CostEstimate(flops=int(time * 10**9), bytes_accessed=0, transcendentals=0)


def ranks(member):
    count = member.shape[1]
    row = lax.broadcasted_iota(jnp.int32, (count, count), 0)
    column = lax.broadcasted_iota(jnp.int32, (count, count), 1)
    earlier = jnp.where(row < column, 1.0, 0.0).astype(jnp.bfloat16)
    seen = jnp.dot(member.astype(jnp.bfloat16), earlier, preferred_element_type=jnp.float32)
    return jnp.sum(seen * member, axis=0, keepdims=True).astype(jnp.int32)


def sorted_columns(bins_row, slab):
    row = lax.broadcasted_iota(jnp.int32, (BINS, BINS), 0)
    column = lax.broadcasted_iota(jnp.int32, (BINS, BINS), 1)
    earlier = jnp.where(row < column, 1.0, 0.0).astype(jnp.bfloat16)
    width = bins_row.shape[1]
    places = lax.broadcasted_iota(jnp.int32, (width, BINS), 0)
    before = jnp.zeros((BINS, 1), jnp.float32)
    choosers = []
    for start in range(0, width, BINS):
        bins = bins_row[:, start : start + BINS]
        member = jnp.where(row == bins, 1.0, 0.0)
        seen = before + jnp.dot(member.astype(jnp.bfloat16), earlier, preferred_element_type=jnp.float32)
        before += jnp.sum(member, axis=1, keepdims=True)
        rank = jnp.sum(seen * member, axis=0, keepdims=True).astype(jnp.int32)
        choosers.append(jnp.where(places == rank * BINS + bins, 1.0, 0.0).astype(jnp.bfloat16))
    return lax.dot_general(
        slab, jnp.concatenate(choosers, axis=1), (((1,), (1,)), ((), ())), preferred_element_type=jnp.float32
    ).astype(jnp.bfloat16)


def projected_rows(queries, projection):
    projected = jnp.dot(queries, projection, preferred_element_type=jnp.float32)
    scale = lax.rsqrt(jnp.sum(projected * projected, axis=1, keepdims=True) + 1e-06)
    return (projected * scale).astype(jnp.bfloat16)


def prepare_kernel(groups, capacity, routes_hbm, queries_hbm, position_ref, *refs):
    piece_refs, (routes_ref, queries_ref, sems) = refs[:groups], refs[groups:]
    copies = [
        pltpu.make_async_copy(routes_hbm, routes_ref, sems.at[0]),
        pltpu.make_async_copy(queries_hbm, queries_ref, sems.at[1]),
    ]
    for copy in copies:
        copy.start()
    requests = queries_ref.shape[0]
    copies[0].wait()
    distance = jnp.bitwise_xor(routes_ref[...], lax.axis_index("db"))
    classes = lax.broadcasted_iota(jnp.int32, (-(-groups // 8) * 8, requests), 0)
    member = jnp.where(classes == distance, 1.0, 0.0)
    position = distance * capacity + ranks(member)
    position_ref[...] = position
    slots = lax.broadcasted_iota(jnp.int32, (groups * capacity, requests), 0)
    chooser = jnp.where(slots == position, 1.0, 0.0).astype(jnp.bfloat16)
    copies[1].wait()
    outgoing = jnp.dot(chooser, queries_ref[...], preferred_element_type=jnp.float32).astype(jnp.bfloat16)
    for i, ref in enumerate(piece_refs):
        ref[...] = outgoing[i * capacity : (i + 1) * capacity]


def prepare(queries, routes, groups, capacity):
    requests, width = queries.shape
    ins = [routes.reshape(1, requests), queries]
    return pl.pallas_call(
        functools.partial(prepare_kernel, groups, capacity),
        out_shape=[jax.ShapeDtypeStruct((1, requests), jnp.int32)]
        + [jax.ShapeDtypeStruct((capacity, width), jnp.bfloat16)] * groups,
        in_specs=[pl.BlockSpec(memory_space=pltpu.HBM)] * len(ins),
        scratch_shapes=[pltpu.VMEM(x.shape, x.dtype) for x in ins] + [pltpu.SemaphoreType.DMA((len(ins),))],
        compiler_params=params(63),
        cost_estimate=us(0),
        name="prepare",
    )(*ins)


def project_kernel(piece_ref, projection_ref, *refs):
    refs[-1][...] = projected_rows(piece_ref[...], projection_ref[...])


def project(piece, projection, *after):
    return pl.pallas_call(
        project_kernel,
        out_shape=jax.ShapeDtypeStruct(piece.shape, jnp.bfloat16),
        in_specs=[pl.BlockSpec(memory_space=pltpu.VMEM)] * 2 + [pl.BlockSpec(memory_space=pl.ANY)] * len(after),
        compiler_params=params(),
        cost_estimate=us(0),
        name="project",
    )(piece, projection, *after)


def sort_kernel(after_ref, bins_ref, slab_ref, sorted_ref):
    sorted_ref[...] = sorted_columns(bins_ref[...], slab_ref[...])


def sort_slab(after, bins, slab):
    return pl.pallas_call(
        sort_kernel,
        out_shape=jax.ShapeDtypeStruct(slab.shape, jnp.bfloat16),
        in_specs=[pl.BlockSpec(memory_space=pl.ANY)] + [pl.BlockSpec(memory_space=pltpu.VMEM)] * 2,
        compiler_params=params(),
        cost_estimate=us(0),
        name="sort_slab",
    )(after, bins.reshape(1, slab.shape[1]), slab)


def sort_and_fetch_kernel(bins_ref, slab_ref, other_hbm, sorted_ref, other_ref, sem):
    copy = pltpu.make_async_copy(other_hbm, other_ref, sem)
    copy.start()
    sorted_ref[...] = sorted_columns(bins_ref[...], slab_ref[...])
    copy.wait()


def sort_and_fetch(bins, slab, other):
    return pl.pallas_call(
        sort_and_fetch_kernel,
        out_shape=[jax.ShapeDtypeStruct(slab.shape, jnp.bfloat16)] * 2,
        in_specs=[pl.BlockSpec(memory_space=pltpu.VMEM)] * 2 + [pl.BlockSpec(memory_space=pltpu.HBM)],
        scratch_shapes=[pltpu.SemaphoreType.DMA],
        compiler_params=params(),
        cost_estimate=us(0),
        name="sort_and_fetch",
    )(bins.reshape(1, slab.shape[1]), slab, other)


def score_kernel(afters, pieces, *refs):
    refs = refs[afters:]
    piece_refs, slab_refs, out_refs = refs[:pieces], refs[pieces : pieces + 2], refs[pieces + 2 :]
    rows = jnp.concatenate([ref[...] for ref in piece_refs], axis=0)
    best = None
    step = 2 * BINS
    for slab_ref in slab_refs:
        for start in range(0, slab_ref.shape[1], step):
            scores = jnp.dot(rows, slab_ref[:, start : start + step], preferred_element_type=jnp.float32)
            for first in range(0, step, BINS):
                part = scores[:, first : first + BINS]
                best = part if best is None else jnp.maximum(best, part)
    count = best.shape[0] // len(out_refs)
    for i, ref in enumerate(out_refs):
        ref[...] = best[i * count : (i + 1) * count]


def score(after, pieces, slabs):
    return pl.pallas_call(
        functools.partial(score_kernel, len(after), len(pieces)),
        out_shape=[jax.ShapeDtypeStruct((piece.shape[0], BINS), jnp.float32) for piece in pieces],
        in_specs=[pl.BlockSpec(memory_space=pl.ANY)] * len(after)
        + [pl.BlockSpec(memory_space=pltpu.VMEM)] * (len(pieces) + len(slabs)),
        compiler_params=params(),
        cost_estimate=us(0),
        name="score",
    )(*after, *pieces, *slabs)


def select_kernel(distances, position_ref, *refs):
    pieces = len(distances)
    first_refs, second_refs, others, out_ref = refs[:pieces], refs[pieces : 2 * pieces], refs[2 * pieces : -1], refs[-1]
    position = position_ref[...]
    parts, choosers = [], []
    for k, first_ref, second_ref in zip(distances, first_refs, second_refs):
        values = jnp.maximum(first_ref[...], second_ref[...])
        high = values.astype(jnp.bfloat16)
        rest = values - high.astype(jnp.float32)
        middle = rest.astype(jnp.bfloat16)
        low = (rest - middle.astype(jnp.float32)).astype(jnp.bfloat16)
        parts.append(jnp.concatenate([high, middle, low], axis=1))
        slots = lax.broadcasted_iota(jnp.int32, (values.shape[0], position.shape[1]), 0)
        choosers.append(jnp.where(slots + k * values.shape[0] == position, 1.0, 0.0).astype(jnp.bfloat16))
    chosen = lax.dot_general(
        jnp.concatenate(choosers, axis=0),
        jnp.concatenate(parts, axis=0),
        (((0,), (0,)), ((), ())),
        preferred_element_type=jnp.float32,
    )
    total = logit_scale * ((chosen[:, :BINS] + chosen[:, BINS : 2 * BINS]) + chosen[:, 2 * BINS :])
    for ref in others:
        total += ref[...]
    out_ref[...] = total


def select(position, distances, answers, others, time):
    flat = [answers[k][i] for i in (0, 1) for k in distances] + others
    return pl.pallas_call(
        functools.partial(select_kernel, distances),
        out_shape=jax.ShapeDtypeStruct((position.shape[1], BINS), jnp.float32),
        in_specs=[pl.BlockSpec(memory_space=pltpu.VMEM)] * (1 + len(flat)),
        compiler_params=params(),
        cost_estimate=us(time),
        name="select",
    )(position, *flat)


def device_paired(queries, projection, vectors, bins, routes):
    groups, slabs = lax.axis_size("db"), lax.axis_size("blk")
    requests = queries.shape[0]
    capacity = 2 * requests // groups

    def along_db(value, distance):
        return lax.ppermute(value, "db", [(i, i ^ distance) for i in range(groups)])

    def along_blk(value, distance):
        return lax.ppermute(value, "blk", [(i, i ^ distance) for i in range(slabs)])

    def along_both(value, distance, distance_blk):
        pairs = [
            (i * slabs + j, (i ^ distance) * slabs + (j ^ distance_blk))
            for i in range(groups)
            for j in range(slabs)
        ]
        return lax.ppermute(value, ("db", "blk"), pairs)

    position, *pieces = prepare(queries, routes, groups, capacity)
    other_slab, other_bins = along_blk(vectors, 1), along_blk(bins, 1)
    arrived = {k: along_db(pieces[k], k) for k in (3, 1, 2)}
    here, partner, answers = {}, {}, {}

    def cross(k, piece, *after):
        here[k] = project(piece, projection, *after)
        partner[k] = along_blk(here[k], 2)

    def scores(k, *after):
        mine, theirs = score(after, [here[k], partner[k]], slabs_here)
        answers[k] = (along_db(mine, k), along_both(theirs, k, 2)) if k else (mine, along_blk(theirs, 2))
        return theirs

    own_slab, fetched = sort_and_fetch(bins, vectors, other_slab)
    slabs_here = [own_slab, sort_slab(position, other_bins, fetched)]
    cross(0, pieces[0], other_bins)
    cross(1, arrived[1], own_slab)
    cross(3, arrived[3])
    done = scores(0)
    cross(2, arrived[2], done)
    done = scores(3, done)
    done = scores(1, done)
    scores(2, done)
    far = select(position, (3,), answers, [], 3)
    return select(position, (0, 1, 2), answers, [far], 0)


def binned_max(query_rows, columns):
    scores = jnp.dot(query_rows, columns, preferred_element_type=jnp.float32)
    return jnp.max(scores.reshape(query_rows.shape[0], -1, BINS), axis=1)


def device_gathered(queries, projection, vectors, bins, routes):
    groups = lax.axis_size("db")
    requests = queries.shape[0]
    capacity = 2 * requests // groups
    slab_width = vectors.shape[1]
    per_bin = slab_width // BINS
    projected = jnp.dot(queries, projection, preferred_element_type=jnp.float32)
    normed = (
        projected * lax.rsqrt(jnp.sum(projected * projected, axis=1, keepdims=True) + 1e-06)
    ).astype(jnp.bfloat16)
    target = routes[:, 0]
    one_hot = (target[:, None] == jnp.arange(groups, dtype=jnp.int32)[None, :]).astype(jnp.int32)
    slot_index = jnp.sum((jnp.cumsum(one_hot, axis=0) - one_hot) * one_hot, axis=1)
    position = target * capacity + slot_index
    chooser = (jnp.arange(groups * capacity, dtype=jnp.int32)[:, None] == position[None, :]).astype(
        jnp.bfloat16
    )
    outgoing = jnp.dot(chooser, normed, preferred_element_type=jnp.float32).astype(jnp.bfloat16)
    arrived = lax.all_to_all(outgoing, "db", split_axis=0, concat_axis=0, tiled=True)
    ordering = jnp.argsort(bins, stable=True).reshape(BINS, per_bin).T.reshape(-1)
    sorted_slab = jnp.take(vectors, ordering, axis=1)
    maxima = binned_max(arrived, lax.all_gather(sorted_slab, "blk", axis=1, tiled=True))
    answers = lax.all_to_all(logit_scale * maxima, "db", split_axis=0, concat_axis=0, tiled=True)
    return jnp.take(answers, position, axis=0)


def solution(mesh):
    paired = mesh.shape["db"] == 4 and mesh.shape["blk"] == 4
    in_specs = (
        P(("parts", "db", "blk"), None),
        P(),
        P(None, ("parts", "db", "blk")),
        P(("parts", "db", "blk")),
        P(("parts", "db", "blk"), None),
    )
    out_specs = P(("parts", "db", "blk"), None)
    return jax.shard_map(
        device_paired if paired else device_gathered,
        mesh=mesh,
        in_specs=in_specs,
        out_specs=out_specs,
        check_vma=False,
    )
```

```python
import functools

import jax
import jax.numpy as jnp
from jax import lax
from jax.experimental import pallas as pl
from jax.experimental.pallas import tpu as pltpu
from jax.sharding import PartitionSpec as P

BINS = 128
logit_scale = 10.0
MIB = 2**20


def params(limit=48):
    return pltpu.CompilerParams(vmem_limit_bytes=limit * MIB)


def us(time):
    return pl.CostEstimate(flops=int(time * 10**9), bytes_accessed=0, transcendentals=0)


def ranks(member):
    count = member.shape[1]
    row = lax.broadcasted_iota(jnp.int32, (count, count), 0)
    column = lax.broadcasted_iota(jnp.int32, (count, count), 1)
    earlier = jnp.where(row < column, 1.0, 0.0).astype(jnp.bfloat16)
    seen = jnp.dot(member.astype(jnp.bfloat16), earlier, preferred_element_type=jnp.float32)
    return jnp.sum(seen * member, axis=0, keepdims=True).astype(jnp.int32)


def sorted_columns(bins_row, slab):
    row = lax.broadcasted_iota(jnp.int32, (BINS, BINS), 0)
    column = lax.broadcasted_iota(jnp.int32, (BINS, BINS), 1)
    earlier = jnp.where(row < column, 1.0, 0.0).astype(jnp.bfloat16)
    width = bins_row.shape[1]
    places = lax.broadcasted_iota(jnp.int32, (width, BINS), 0)
    before = jnp.zeros((BINS, 1), jnp.float32)
    choosers = []
    for start in range(0, width, BINS):
        bins = bins_row[:, start : start + BINS]
        member = jnp.where(row == bins, 1.0, 0.0)
        seen = before + jnp.dot(member.astype(jnp.bfloat16), earlier, preferred_element_type=jnp.float32)
        before += jnp.sum(member, axis=1, keepdims=True)
        rank = jnp.sum(seen * member, axis=0, keepdims=True).astype(jnp.int32)
        choosers.append(jnp.where(places == rank * BINS + bins, 1.0, 0.0).astype(jnp.bfloat16))
    return lax.dot_general(
        slab, jnp.concatenate(choosers, axis=1), (((1,), (1,)), ((), ())), preferred_element_type=jnp.float32
    ).astype(jnp.bfloat16)


def projected_rows(queries, projection):
    projected = jnp.dot(queries, projection, preferred_element_type=jnp.float32)
    scale = lax.rsqrt(jnp.sum(projected * projected, axis=1, keepdims=True) + 1e-06)
    return (projected * scale).astype(jnp.bfloat16)


def prepare_kernel(groups, capacity, routes_hbm, queries_hbm, position_ref, *refs):
    piece_refs, (routes_ref, queries_ref, sems) = refs[:groups], refs[groups:]
    copies = [
        pltpu.make_async_copy(routes_hbm, routes_ref, sems.at[0]),
        pltpu.make_async_copy(queries_hbm, queries_ref, sems.at[1]),
    ]
    for copy in copies:
        copy.start()
    requests = queries_ref.shape[0]
    copies[0].wait()
    distance = jnp.bitwise_xor(routes_ref[...], lax.axis_index("db"))
    classes = lax.broadcasted_iota(jnp.int32, (-(-groups // 8) * 8, requests), 0)
    member = jnp.where(classes == distance, 1.0, 0.0)
    position = distance * capacity + ranks(member)
    position_ref[...] = position
    slots = lax.broadcasted_iota(jnp.int32, (groups * capacity, requests), 0)
    chooser = jnp.where(slots == position, 1.0, 0.0).astype(jnp.bfloat16)
    copies[1].wait()
    outgoing = jnp.dot(chooser, queries_ref[...], preferred_element_type=jnp.float32).astype(jnp.bfloat16)
    for i, ref in enumerate(piece_refs):
        ref[...] = outgoing[i * capacity : (i + 1) * capacity]


def prepare(queries, routes, groups, capacity):
    requests, width = queries.shape
    ins = [routes.reshape(1, requests), queries]
    return pl.pallas_call(
        functools.partial(prepare_kernel, groups, capacity),
        out_shape=[jax.ShapeDtypeStruct((1, requests), jnp.int32)]
        + [jax.ShapeDtypeStruct((capacity, width), jnp.bfloat16)] * groups,
        in_specs=[pl.BlockSpec(memory_space=pltpu.HBM)] * len(ins),
        scratch_shapes=[pltpu.VMEM(x.shape, x.dtype) for x in ins] + [pltpu.SemaphoreType.DMA((len(ins),))],
        compiler_params=params(63),
        cost_estimate=us(0),
        name="prepare",
    )(*ins)


def project_kernel(piece_ref, projection_ref, *refs):
    refs[-1][...] = projected_rows(piece_ref[...], projection_ref[...])


def project(piece, projection, *after):
    return pl.pallas_call(
        project_kernel,
        out_shape=jax.ShapeDtypeStruct(piece.shape, jnp.bfloat16),
        in_specs=[pl.BlockSpec(memory_space=pltpu.VMEM)] * 2 + [pl.BlockSpec(memory_space=pl.ANY)] * len(after),
        compiler_params=params(),
        cost_estimate=us(0),
        name="project",
    )(piece, projection, *after)


def sort_kernel(after_ref, bins_ref, slab_ref, sorted_ref):
    sorted_ref[...] = sorted_columns(bins_ref[...], slab_ref[...])


def sort_slab(after, bins, slab):
    return pl.pallas_call(
        sort_kernel,
        out_shape=jax.ShapeDtypeStruct(slab.shape, jnp.bfloat16),
        in_specs=[pl.BlockSpec(memory_space=pl.ANY)] + [pl.BlockSpec(memory_space=pltpu.VMEM)] * 2,
        compiler_params=params(),
        cost_estimate=us(0),
        name="sort_slab",
    )(after, bins.reshape(1, slab.shape[1]), slab)


def sort_and_fetch_kernel(bins_ref, slab_ref, other_hbm, sorted_ref, other_ref, sem):
    copy = pltpu.make_async_copy(other_hbm, other_ref, sem)
    copy.start()
    sorted_ref[...] = sorted_columns(bins_ref[...], slab_ref[...])
    copy.wait()


def sort_and_fetch(bins, slab, other):
    return pl.pallas_call(
        sort_and_fetch_kernel,
        out_shape=[jax.ShapeDtypeStruct(slab.shape, jnp.bfloat16)] * 2,
        in_specs=[pl.BlockSpec(memory_space=pltpu.VMEM)] * 2 + [pl.BlockSpec(memory_space=pltpu.HBM)],
        scratch_shapes=[pltpu.SemaphoreType.DMA],
        compiler_params=params(),
        cost_estimate=us(0),
        name="sort_and_fetch",
    )(bins.reshape(1, slab.shape[1]), slab, other)


def score_kernel(afters, pieces, *refs):
    refs = refs[afters:]
    piece_refs, slab_refs, out_refs = refs[:pieces], refs[pieces : pieces + 2], refs[pieces + 2 :]
    rows = jnp.concatenate([ref[...] for ref in piece_refs], axis=0)
    best = None
    step = 2 * BINS
    for slab_ref in slab_refs:
        for start in range(0, slab_ref.shape[1], step):
            scores = jnp.dot(rows, slab_ref[:, start : start + step], preferred_element_type=jnp.float32)
            for first in range(0, step, BINS):
                part = scores[:, first : first + BINS]
                best = part if best is None else jnp.maximum(best, part)
    count = best.shape[0] // len(out_refs)
    for i, ref in enumerate(out_refs):
        ref[...] = best[i * count : (i + 1) * count]


def score(after, pieces, slabs):
    return pl.pallas_call(
        functools.partial(score_kernel, len(after), len(pieces)),
        out_shape=[jax.ShapeDtypeStruct((piece.shape[0], BINS), jnp.float32) for piece in pieces],
        in_specs=[pl.BlockSpec(memory_space=pl.ANY)] * len(after)
        + [pl.BlockSpec(memory_space=pltpu.VMEM)] * (len(pieces) + len(slabs)),
        compiler_params=params(),
        cost_estimate=us(0),
        name="score",
    )(*after, *pieces, *slabs)


def select_kernel(distances, position_ref, *refs):
    pieces = len(distances)
    first_refs, second_refs, others, out_ref = refs[:pieces], refs[pieces : 2 * pieces], refs[2 * pieces : -1], refs[-1]
    position = position_ref[...]
    parts, choosers = [], []
    for k, first_ref, second_ref in zip(distances, first_refs, second_refs):
        values = jnp.maximum(first_ref[...], second_ref[...])
        high = values.astype(jnp.bfloat16)
        rest = values - high.astype(jnp.float32)
        middle = rest.astype(jnp.bfloat16)
        low = (rest - middle.astype(jnp.float32)).astype(jnp.bfloat16)
        parts.append(jnp.concatenate([high, middle, low], axis=1))
        slots = lax.broadcasted_iota(jnp.int32, (values.shape[0], position.shape[1]), 0)
        choosers.append(jnp.where(slots + k * values.shape[0] == position, 1.0, 0.0).astype(jnp.bfloat16))
    chosen = lax.dot_general(
        jnp.concatenate(choosers, axis=0),
        jnp.concatenate(parts, axis=0),
        (((0,), (0,)), ((), ())),
        preferred_element_type=jnp.float32,
    )
    total = logit_scale * ((chosen[:, :BINS] + chosen[:, BINS : 2 * BINS]) + chosen[:, 2 * BINS :])
    for ref in others:
        total += ref[...]
    out_ref[...] = total


def select(position, distances, answers, others, time):
    flat = [answers[k][i] for i in (0, 1) for k in distances] + others
    return pl.pallas_call(
        functools.partial(select_kernel, distances),
        out_shape=jax.ShapeDtypeStruct((position.shape[1], BINS), jnp.float32),
        in_specs=[pl.BlockSpec(memory_space=pltpu.VMEM)] * (1 + len(flat)),
        compiler_params=params(),
        cost_estimate=us(time),
        name="select",
    )(position, *flat)


def device_paired(queries, projection, vectors, bins, routes):
    groups, slabs = lax.axis_size("db"), lax.axis_size("blk")
    requests = queries.shape[0]
    capacity = 2 * requests // groups

    def along_db(value, distance):
        return lax.ppermute(value, "db", [(i, i ^ distance) for i in range(groups)])

    def along_blk(value, distance):
        return lax.ppermute(value, "blk", [(i, i ^ distance) for i in range(slabs)])

    def along_both(value, distance, distance_blk):
        pairs = [
            (i * slabs + j, (i ^ distance) * slabs + (j ^ distance_blk))
            for i in range(groups)
            for j in range(slabs)
        ]
        return lax.ppermute(value, ("db", "blk"), pairs)

    position, *pieces = prepare(queries, routes, groups, capacity)
    other_slab, other_bins = along_blk(vectors, 1), along_blk(bins, 1)
    arrived = {k: along_db(pieces[k], k) for k in (3, 1, 2)}
    here, partner, answers = {}, {}, {}

    def cross(k, piece, *after):
        here[k] = project(piece, projection, *after)
        partner[k] = along_blk(here[k], 2)

    def scores(k, *after):
        mine, theirs = score(after, [here[k], partner[k]], slabs_here)
        answers[k] = (along_db(mine, k), along_both(theirs, k, 2)) if k else (mine, along_blk(theirs, 2))
        return theirs

    own_slab, fetched = sort_and_fetch(bins, vectors, other_slab)
    slabs_here = [own_slab, sort_slab(position, other_bins, fetched)]
    cross(0, pieces[0], own_slab)
    cross(1, arrived[1], own_slab)
    cross(3, arrived[3])
    done = scores(0)
    cross(2, arrived[2], done)
    done = scores(3, done)
    done = scores(1, done)
    scores(2, done)
    far = select(position, (3,), answers, [], 3)
    return select(position, (0, 1, 2), answers, [far], 0)


def binned_max(query_rows, columns):
    scores = jnp.dot(query_rows, columns, preferred_element_type=jnp.float32)
    return jnp.max(scores.reshape(query_rows.shape[0], -1, BINS), axis=1)


def device_gathered(queries, projection, vectors, bins, routes):
    groups = lax.axis_size("db")
    requests = queries.shape[0]
    capacity = 2 * requests // groups
    slab_width = vectors.shape[1]
    per_bin = slab_width // BINS
    projected = jnp.dot(queries, projection, preferred_element_type=jnp.float32)
    normed = (
        projected * lax.rsqrt(jnp.sum(projected * projected, axis=1, keepdims=True) + 1e-06)
    ).astype(jnp.bfloat16)
    target = routes[:, 0]
    one_hot = (target[:, None] == jnp.arange(groups, dtype=jnp.int32)[None, :]).astype(jnp.int32)
    slot_index = jnp.sum((jnp.cumsum(one_hot, axis=0) - one_hot) * one_hot, axis=1)
    position = target * capacity + slot_index
    chooser = (jnp.arange(groups * capacity, dtype=jnp.int32)[:, None] == position[None, :]).astype(
        jnp.bfloat16
    )
    outgoing = jnp.dot(chooser, normed, preferred_element_type=jnp.float32).astype(jnp.bfloat16)
    arrived = lax.all_to_all(outgoing, "db", split_axis=0, concat_axis=0, tiled=True)
    ordering = jnp.argsort(bins, stable=True).reshape(BINS, per_bin).T.reshape(-1)
    sorted_slab = jnp.take(vectors, ordering, axis=1)
    maxima = binned_max(arrived, lax.all_gather(sorted_slab, "blk", axis=1, tiled=True))
    answers = lax.all_to_all(logit_scale * maxima, "db", split_axis=0, concat_axis=0, tiled=True)
    return jnp.take(answers, position, axis=0)


def solution(mesh):
    paired = mesh.shape["db"] == 4 and mesh.shape["blk"] == 4
    in_specs = (
        P(("parts", "db", "blk"), None),
        P(),
        P(None, ("parts", "db", "blk")),
        P(("parts", "db", "blk")),
        P(("parts", "db", "blk"), None),
    )
    out_specs = P(("parts", "db", "blk"), None)
    return jax.shard_map(
        device_paired if paired else device_gathered,
        mesh=mesh,
        in_specs=in_specs,
        out_specs=out_specs,
        check_vma=False,
    )
```
